32 devices in a mesh: clip: 8 (over z, x), grp: 4 (over y, core).
Axes of the slice: x: 2, y: 2, z: 4, core: 2. Of those that a mesh axis runs over, the one named last changes fastest.
Arguments:
- hidden: bfloat16 [8, 20, 256, 1152], P('clip', 'grp'), may hold values from -6 to 6
- modulation: float32 [8, 3, 1152], P('clip'), may hold values from -3 to 3
- clip_frames: int32 [8], P('clip'), may hold values from 1 to 20, as said below
- qkv_weight: bfloat16 [1152, 3456], P(None, ('clip', 'grp')), may hold values from -0.1875 to 0.1875
- out_weight: bfloat16 [1152, 1152], P(None, ('clip', 'grp')), may hold values from -0.1875 to 0.1875
Outputs:
- output: bfloat16 [8, 20, 256, 1152], P('clip', 'grp')
The draws below stay inside these ranges and needn't reach their ends.
Inputs may be any that keep to these rules, and one draw needn't show every extreme that they name: `clip_frames`: at least one clip has all 20 frames.
All inputs are finite; a program needn't handle non-finite values.
Results may differ from the reference program's by a relative error of at most 0.0085.
Values may be sent and summed in bfloat16 or wider, within the bound.
A program may use at most 128 MiB of HBM per device.

```python
import jax
import jax.numpy as jnp
from jax import lax

D = 1152
HEADS = 16
HEAD_DIM = 72
FRAMES = 20
TOK_FRAME = 256
CLIPS = 8


def draw_clip_frames(key, part):
    counts = jax.random.randint(jax.random.fold_in(key, 1), (CLIPS,), 1, FRAMES + 1)
    chosen = jax.random.randint(jax.random.fold_in(key, 2), (), 0, CLIPS)
    return jnp.where(jnp.arange(CLIPS) == chosen, FRAMES, counts).astype(jnp.int32)


def shard_levels(key, shape, pieces, smallest, largest):
    level, own = 1.0, jax.random.fold_in(key, 6)
    for position, parts in pieces:
        draws = jnp.exp(jax.random.uniform(jax.random.fold_in(own, position), (parts,), jnp.float32, smallest / len(pieces), largest / len(pieces)))
        level = level * jnp.repeat(draws, shape[position] // parts).reshape([-1 if axis == position else 1 for axis in range(len(shape))])
    return level


def noise(key, shape, scale, limit, split=(), kind=jnp.bfloat16):
    result = jax.random.normal(key, shape, jnp.float32) * scale
    if len(split) > 0:
        result = shard_levels(key, shape, split, -0.22, 0.18) * result
    return jnp.clip(result, min=-limit, max=limit).astype(kind)


def setup_inputs(seed: int = 0) -> dict:
    streams_of = jax.random.split(jax.random.key(seed), 6)
    hidden = noise(streams_of[0], (CLIPS, FRAMES, TOK_FRAME, D), 1.0, 6.0, ((0, 8), (1, 4)))
    modulation = noise(streams_of[1], (CLIPS, 3, D), 0.5, 3.0, ((0, 8),), jnp.float32)
    clip_frames = draw_clip_frames(jax.random.fold_in(streams_of[5], 71), 0)
    qkv_weight = noise(streams_of[3], (D, 3 * D), D ** -0.5, 0.1875, ((1, 32),))
    out_weight = noise(streams_of[4], (D, D), D ** -0.5, 0.1875, ((1, 32),))
    return dict(hidden=hidden, modulation=modulation, clip_frames=clip_frames, qkv_weight=qkv_weight, out_weight=out_weight)


def modulate(features, table):
    average = lax.optimization_barrier(jnp.mean(features, axis=-1, keepdims=True))
    centred = features - average
    variance = lax.optimization_barrier(jnp.mean(centred * centred, axis=-1, keepdims=True))
    normed = centred * lax.rsqrt(variance + 1e-06)
    return (normed * (1.0 + table[1]) + table[0]).astype(jnp.bfloat16)

def reference(hidden, modulation, clip_frames, qkv_weight, out_weight):

    def one_clip(inputs):
        frames_in, table, length = inputs
        features = frames_in.astype(jnp.float32)
        modulated = modulate(features, table)
        qkv_rows = jnp.dot(modulated.reshape(FRAMES * TOK_FRAME, D), qkv_weight, preferred_element_type=jnp.float32).astype(jnp.bfloat16)
        qkv_rows = qkv_rows.reshape(FRAMES, TOK_FRAME, 3 * D)
        query_heads = qkv_rows[:, :, :D].reshape(FRAMES, TOK_FRAME, HEADS, HEAD_DIM).astype(jnp.float32)
        key_heads = qkv_rows[:, :, D:2 * D].reshape(FRAMES, TOK_FRAME, HEADS, HEAD_DIM).astype(jnp.float32)
        value_heads = qkv_rows[:, :, 2 * D:].reshape(FRAMES, TOK_FRAME, HEADS, HEAD_DIM).astype(jnp.float32)
        scores = jnp.einsum('fshd,gshd->hfgs', query_heads, key_heads) * HEAD_DIM ** (-0.5)
        key_live = jnp.arange(FRAMES) < length
        scores = jnp.where(key_live[None, None, :, None], scores, -1e+30)
        attn_weights = jax.nn.softmax(scores, axis=2).astype(jnp.bfloat16)
        mixed = jnp.einsum('hfgs,gshd->fshd', attn_weights.astype(jnp.float32), value_heads).astype(jnp.bfloat16)
        mixed = mixed.reshape(FRAMES * TOK_FRAME, D)
        projected = jnp.dot(mixed, out_weight, preferred_element_type=jnp.float32).reshape(FRAMES, TOK_FRAME, D)
        frame_live = (jnp.arange(FRAMES) < length).astype(jnp.float32)
        return (features + table[2] * projected * frame_live[:, None, None]).astype(jnp.bfloat16)
    return lax.map(one_clip, (hidden, modulation, clip_frames))
```

```python
import functools

import jax
import jax.numpy as jnp
from jax import lax
from jax.experimental import pallas as pl
from jax.experimental.pallas import tpu as pltpu
from jax.sharding import PartitionSpec as P

HEADS = 16
HALF = 8
PAIR = 16
LOG2E = 1.4426950408889634
NT = (((1,), (1,)), ((), ()))


def col_tile(cols):
    return 384 if cols % 384 == 0 else 128


def make_bias(bias_ref, length):
    keys = bias_ref.shape[1]
    row = lax.broadcasted_iota(jnp.int32, bias_ref.shape, 0)
    col = lax.broadcasted_iota(jnp.int32, bias_ref.shape, 1)
    same = (row % HALF) == (col % HALF)
    live = (col // HALF) < length
    bias_ref[...] = jnp.where(same & live, 0.0, -1e30).astype(jnp.float32)


def modulate_step(step, x_ref, table_ref, mod_ref):
    frames, tokens, width = x_ref.shape
    pairs = frames // 2
    block = step // pairs
    pair = step % pairs
    x = x_ref[pl.ds(2 * pair, 2), pl.ds(PAIR * block, PAIR), :].astype(jnp.float32)
    mean = jnp.sum(x, axis=-1, keepdims=True) * (1.0 / width)
    centred = x - mean
    var = jnp.sum(centred * centred, axis=-1, keepdims=True) * (1.0 / width)
    normed = centred * lax.rsqrt(var + 1e-06)
    y = normed * (1.0 + table_ref[1:2, :])[None] + table_ref[0:1, :][None]
    for half in range(2):
        part = y[:, half * HALF : (half + 1) * HALF, :].reshape(2 * HALF, width)
        start = pl.multiple_of((2 * block + half) * frames * HALF + pair * 2 * HALF, 16)
        mod_ref[pl.ds(start, 2 * HALF), :] = part.astype(jnp.bfloat16)


def qkv_step(step, mod_ref, wqkv_ref, qkv_ref, rows, first=0):
    count = mod_ref.shape[0] // rows
    tile = col_tile(wqkv_ref.shape[0])
    n = pl.multiple_of((first + step // count) * tile, 128)
    m = pl.multiple_of((step % count) * rows, 16)
    got = lax.dot_general(
        mod_ref[pl.ds(m, rows), :], wqkv_ref[pl.ds(n, tile), :], NT,
        preferred_element_type=jnp.float32,
    )
    qkv_ref[pl.ds(m, rows), pl.ds(n, tile)] = got.astype(jnp.bfloat16)


def attend(start, rows, width, qkv_ref, bias_ref, mixed_ref, mixed_start):
    head = width // HEADS
    scale = head**-0.5 * LOG2E
    tiles = [None] * (width // 128)
    for h in range(HEADS):
        low, high = h * head, (h + 1) * head
        w0 = low // 128 * 128
        w1 = (high + 127) // 128 * 128
        lane = lax.broadcasted_iota(jnp.int32, (1, w1 - w0), 1) + w0
        inside = (lane >= low) & (lane < high)
        q = qkv_ref[pl.ds(start, rows), w0:w1]
        k = qkv_ref[pl.ds(start, rows), width + w0 : width + w1]
        v = qkv_ref[pl.ds(start, rows), 2 * width + w0 : 2 * width + w1]
        q = q * jnp.where(inside, 1.0, 0.0).astype(jnp.bfloat16)
        s = lax.dot_general(q, k, NT, preferred_element_type=jnp.float32)
        s = s * scale + bias_ref[...]
        p = jnp.exp2(s - jnp.max(s, axis=-1, keepdims=True))
        total = jnp.sum(p, axis=-1, keepdims=True)
        o = jnp.dot(p.astype(jnp.bfloat16), v, preferred_element_type=jnp.float32)
        o = o * (1.0 / total)
        for t in range(w0 // 128, w1 // 128):
            part = o[:, t * 128 - w0 : t * 128 - w0 + 128]
            where = inside[:, t * 128 - w0 : t * 128 - w0 + 128]
            tiles[t] = part if tiles[t] is None else jnp.where(where, part, tiles[t])
            if high >= (t + 1) * 128:
                mixed_ref[pl.ds(mixed_start, rows), t * 128 : (t + 1) * 128] = tiles[t].astype(
                    jnp.bfloat16
                )


def finish_block(block, x_ref, table_ref, length, qkv_ref, bias_ref, mixed_ref, proj_ref, wout_ref, out_ref):
    frames, tokens, width = x_ref.shape
    rows = frames * HALF

    def half_step(half, carry):
        start = pl.multiple_of((2 * block + half) * rows, 16)
        attend(start, rows, width, qkv_ref, bias_ref, mixed_ref, pl.multiple_of(half * rows, 16))
        return carry

    lax.fori_loop(0, 2, half_step, 0)
    tile = col_tile(width)
    def project(n, carry):
        at = pl.multiple_of(n * tile, 128)
        proj_ref[:, pl.ds(at, tile)] = lax.dot_general(
            mixed_ref[...], wout_ref[pl.ds(at, tile), :], NT, preferred_element_type=jnp.float32
        )
        return carry

    lax.fori_loop(0, width // tile, project, 0)
    gate = table_ref[2:3, :]

    def close(f, carry):
        at = pl.multiple_of(f * HALF, HALF)
        top = proj_ref[pl.ds(at, HALF), :]
        low = proj_ref[pl.ds(pl.multiple_of(rows + at, HALF), HALF), :]
        got = jnp.concatenate([top, low], axis=0)
        live = jnp.where(f < length, 1.0, 0.0).astype(jnp.float32)
        x = x_ref[f, pl.ds(pl.multiple_of(PAIR * block, PAIR), PAIR), :].astype(jnp.float32)
        out_ref[f, pl.ds(pl.multiple_of(PAIR * block, PAIR), PAIR), :] = (
            x + gate * got * live
        ).astype(jnp.bfloat16)
        return carry

    lax.fori_loop(0, frames, close, 0)


def kernel(len_ref, x_ref, table_ref, wqkv_ref, wout_ref, out_ref, mod_ref, qkv_ref, bias_ref, mixed_ref, proj_ref):
    frames, tokens, width = x_ref.shape
    length = len_ref[0]
    make_bias(bias_ref, length)

    def first(step, carry):
        modulate_step(step, x_ref, table_ref, mod_ref)
        return carry

    lax.fori_loop(0, frames // 2 * (tokens // PAIR), first, 0)
    rows = 2 * frames * HALF

    def second(step, carry):
        qkv_step(step, mod_ref, wqkv_ref, qkv_ref, rows)
        return carry

    lax.fori_loop(0, (mod_ref.shape[0] // rows) * (3 * width // col_tile(3 * width)), second, 0)

    def third(block, carry):
        finish_block(block, x_ref, table_ref, length, qkv_ref, bias_ref, mixed_ref, proj_ref, wout_ref, out_ref)
        return carry

    lax.fori_loop(0, tokens // PAIR, third, 0)


def on_device(hidden, modulation, clip_frames, qkv_weight, out_weight):
    both = ("clip", "grp")
    wqkv = lax.all_gather(qkv_weight.T, both, axis=0, tiled=True)
    wout = lax.all_gather(out_weight.T, both, axis=0, tiled=True)
    x = lax.all_to_all(hidden[0], "grp", split_axis=1, concat_axis=0, tiled=True)
    frames, tokens, width = x.shape
    rows = frames * HALF
    vmem = pl.BlockSpec(memory_space=pltpu.VMEM)
    out = pl.pallas_call(
        kernel,
        out_shape=jax.ShapeDtypeStruct(x.shape, jnp.bfloat16),
        in_specs=[pl.BlockSpec(memory_space=pltpu.SMEM)] + [vmem] * 4,
        out_specs=vmem,
        scratch_shapes=[
            pltpu.VMEM((frames * tokens, width), jnp.bfloat16),
            pltpu.VMEM((frames * tokens, 3 * width), jnp.bfloat16),
            pltpu.VMEM((rows, rows), jnp.float32),
            pltpu.VMEM((2 * rows, width), jnp.bfloat16),
            pltpu.VMEM((2 * rows, width), jnp.float32),
        ],
        compiler_params=pltpu.CompilerParams(vmem_limit_bytes=56 * 1024 * 1024),
    )(clip_frames, x, modulation[0], wqkv, wout)
    return lax.all_to_all(out, "grp", split_axis=0, concat_axis=1, tiled=True)[None]


def solution(mesh):
    placed = (
        P("clip", "grp", None, None),
        P("clip", None, None),
        P("clip"),
        P(None, ("clip", "grp")),
        P(None, ("clip", "grp")),
    )
    return jax.shard_map(
        on_device,
        mesh=mesh,
        in_specs=placed,
        out_specs=P("clip", "grp", None, None),
        check_vma=False,
    )
```

```python
import functools

import jax
import jax.numpy as jnp
from jax import lax
from jax.experimental import pallas as pl
from jax.experimental.pallas import tpu as pltpu
from jax.sharding import PartitionSpec as P

HEADS = 16
HALF = 8
PAIR = 16
LOG2E = 1.4426950408889634
NT = (((1,), (1,)), ((), ()))


def col_tile(cols):
    return 384 if cols % 384 == 0 else 128


def make_bias(bias_ref, length):
    keys = bias_ref.shape[1]
    row = lax.broadcasted_iota(jnp.int32, bias_ref.shape, 0)
    col = lax.broadcasted_iota(jnp.int32, bias_ref.shape, 1)
    same = (row % HALF) == (col % HALF)
    live = (col // HALF) < length
    bias_ref[...] = jnp.where(same & live, 0.0, -1e30).astype(jnp.float32)


def modulate_step(step, x_ref, table_ref, mod_ref):
    frames, tokens, width = x_ref.shape
    pairs = frames // 2
    block = step // pairs
    pair = step % pairs
    x = x_ref[pl.ds(2 * pair, 2), pl.ds(PAIR * block, PAIR), :].astype(jnp.float32)
    mean = jnp.sum(x, axis=-1, keepdims=True) * (1.0 / width)
    centred = x - mean
    var = jnp.sum(centred * centred, axis=-1, keepdims=True) * (1.0 / width)
    normed = centred * lax.rsqrt(var + 1e-06)
    y = normed * (1.0 + table_ref[1:2, :])[None] + table_ref[0:1, :][None]
    for half in range(2):
        part = y[:, half * HALF : (half + 1) * HALF, :].reshape(2 * HALF, width)
        start = pl.multiple_of((2 * block + half) * frames * HALF + pair * 2 * HALF, 16)
        mod_ref[pl.ds(start, 2 * HALF), :] = part.astype(jnp.bfloat16)


def qkv_step(step, mod_ref, wqkv_ref, qkv_ref, rows, first=0):
    count = mod_ref.shape[0] // rows
    tile = col_tile(wqkv_ref.shape[0])
    n = pl.multiple_of((first + step // count) * tile, 128)
    m = pl.multiple_of((step % count) * rows, 16)
    got = lax.dot_general(
        mod_ref[pl.ds(m, rows), :], wqkv_ref[pl.ds(n, tile), :], NT,
        preferred_element_type=jnp.float32,
    )
    qkv_ref[pl.ds(m, rows), pl.ds(n, tile)] = got.astype(jnp.bfloat16)


def attend(start, rows, width, qkv_ref, bias_ref, mixed_ref, mixed_start):
    head = width // HEADS
    scale = head**-0.5 * LOG2E
    tiles = [None] * (width // 128)
    for h in range(HEADS):
        low, high = h * head, (h + 1) * head
        w0 = low // 128 * 128
        w1 = (high + 127) // 128 * 128
        lane = lax.broadcasted_iota(jnp.int32, (1, w1 - w0), 1) + w0
        inside = (lane >= low) & (lane < high)
        q = qkv_ref[pl.ds(start, rows), w0:w1]
        k = qkv_ref[pl.ds(start, rows), width + w0 : width + w1]
        v = qkv_ref[pl.ds(start, rows), 2 * width + w0 : 2 * width + w1]
        q = q * jnp.where(inside, 1.0, 0.0).astype(jnp.bfloat16)
        s = lax.dot_general(q, k, NT, preferred_element_type=jnp.float32)
        s = s * scale + bias_ref[...]
        p = jnp.exp2(s - jnp.max(s, axis=-1, keepdims=True))
        total = jnp.sum(p, axis=-1, keepdims=True)
        o = jnp.dot(p.astype(jnp.bfloat16), v, preferred_element_type=jnp.float32)
        o = o * (1.0 / total)
        for t in range(w0 // 128, w1 // 128):
            part = o[:, t * 128 - w0 : t * 128 - w0 + 128]
            where = inside[:, t * 128 - w0 : t * 128 - w0 + 128]
            tiles[t] = part if tiles[t] is None else jnp.where(where, part, tiles[t])
            if high >= (t + 1) * 128:
                mixed_ref[pl.ds(mixed_start, rows), t * 128 : (t + 1) * 128] = tiles[t].astype(
                    jnp.bfloat16
                )


def finish_block(block, x_ref, table_ref, length, qkv_ref, bias_ref, mixed_ref, proj_ref, wout_ref, out_ref):
    frames, tokens, width = x_ref.shape
    rows = frames * HALF

    def half_step(half, carry):
        start = pl.multiple_of((2 * block + half) * rows, 16)
        attend(start, rows, width, qkv_ref, bias_ref, mixed_ref, pl.multiple_of(half * rows, 16))
        return carry

    lax.fori_loop(0, 2, half_step, 0)
    tile = col_tile(width)
    def project(n, carry):
        at = pl.multiple_of(n * tile, 128)
        proj_ref[:, pl.ds(at, tile)] = lax.dot_general(
            mixed_ref[...], wout_ref[pl.ds(at, tile), :], NT, preferred_element_type=jnp.float32
        )
        return carry

    lax.fori_loop(0, width // tile, project, 0)
    gate = table_ref[2:3, :]

    def close(f, carry):
        at = pl.multiple_of(f * HALF, HALF)
        top = proj_ref[pl.ds(at, HALF), :]
        low = proj_ref[pl.ds(pl.multiple_of(rows + at, HALF), HALF), :]
        got = jnp.concatenate([top, low], axis=0)
        live = jnp.where(f < length, 1.0, 0.0).astype(jnp.float32)
        x = x_ref[f, pl.ds(pl.multiple_of(PAIR * block, PAIR), PAIR), :].astype(jnp.float32)
        out_ref[f, pl.ds(pl.multiple_of(PAIR * block, PAIR), PAIR), :] = (
            x + gate * got * live
        ).astype(jnp.bfloat16)
        return carry

    lax.fori_loop(0, frames, close, 0)


def ceil16(n):
    return (n + 15) // 16 * 16


def kernel(
    sizes, len_ref, hid_ref, table_ref, shard_ref, out_ref,
    x_ref, w_ref, stage_ref, wqkv_ref, wout_ref, mod_ref, qkv_ref, bias_ref, mixed_ref, proj_ref, done_ref,
    local_sem, y_send, y_recv, right_send, right_recv, left_send, left_recv, x_send, x_recv, k_send, k_recv,
    in_send, in_recv, back_send, back_recv, back_local,
):
    zs, ys, group, shard_rows, qkv_rows, out_rows, clips_step = sizes
    own, all_tokens, width = hid_ref.shape
    frames, tokens, _ = x_ref.shape
    blocks = tokens // PAIR
    clip, grp = lax.axis_index("clip"), lax.axis_index("grp")
    z, x = clip // 2, clip % 2
    y, k = grp // 2, grp % 2
    mesh_ids = pl.DeviceIdType.MESH
    length = len_ref[0]

    def mate(step):
        return lax.rem(grp + step, group)

    def at(z_to, x_to):
        return (z_to * 2 + x_to, grp)

    barrier = pltpu.get_barrier_semaphore()
    for step in range(1, group):
        pl.semaphore_signal(barrier, inc=1, device_id=(clip, mate(step)), device_id_type=mesh_ids)
    pl.semaphore_signal(barrier, inc=1, device_id=at(z, 1 - x), device_id_type=mesh_ids)

    @pl.when(z > 0)
    def _():
        pl.semaphore_signal(barrier, inc=1, device_id=at(z - 1, x), device_id_type=mesh_ids)

    @pl.when(z < zs - 1)
    def _():
        pl.semaphore_signal(barrier, inc=1, device_id=at(z + 1, x), device_id_type=mesh_ids)

    own_w = pltpu.make_async_copy(
        shard_ref, w_ref.at[z, x, k, pl.ds(pl.multiple_of(y * shard_rows, 16), shard_rows)], local_sem.at[0]
    )
    own_w.start()
    own_x = pltpu.make_async_copy(
        hid_ref.at[:, pl.ds(pl.multiple_of(grp * tokens, PAIR), tokens)],
        x_ref.at[pl.ds(grp * own, own)], local_sem.at[1],
    )
    own_x.start()
    ends = jnp.where(z > 0, 1, 0) + jnp.where(z < zs - 1, 1, 0)
    pl.semaphore_wait(barrier, group + ends)

    def remote(src, dst, send, recv, to):
        return pltpu.make_async_remote_copy(
            src_ref=src, dst_ref=dst, send_sem=send, recv_sem=recv, device_id=to, device_id_type=mesh_ids
        )

    def y_copy(step):
        rows = pl.ds(pl.multiple_of(y * shard_rows, 16), shard_rows)
        to = (clip, lax.rem(y + step, ys) * 2 + k)
        return remote(shard_ref, w_ref.at[z, x, k, rows], y_send.at[step], y_recv.at[step], to)

    def in_copy(step):
        to = mate(step)
        src = hid_ref.at[:, pl.ds(pl.multiple_of(to * tokens, PAIR), tokens)]
        return remote(src, x_ref.at[pl.ds(grp * own, own)], in_send.at[step], in_recv.at[step], (clip, to))

    def right_copy(origin, hop):
        slot = w_ref.at[origin, x, k]
        return remote(slot, slot, right_send.at[hop], right_recv.at[hop], at(z + 1, x))

    def left_copy(origin, hop):
        slot = w_ref.at[origin, x, k]
        return remote(slot, slot, left_send.at[hop], left_recv.at[hop], at(z - 1, x))

    def x_copy(origin):
        slot = w_ref.at[origin, x, k]
        return remote(slot, slot, x_send.at[origin], x_recv.at[origin], at(z, 1 - x))

    def k_copy(origin, x_of):
        slot = w_ref.at[origin, x_of, k]
        return remote(slot, slot, k_send.at[x_of, origin], k_recv.at[x_of, origin], (clip, y * 2 + 1 - k))

    for step in range(1, ys):
        y_copy(step).start()
    own_w.wait()
    for step in range(1, group):
        in_copy(step).start()
    make_bias(bias_ref, length)
    for step in range(1, ys):
        y_copy(step).wait_recv()

    x_copy(z).start()

    @pl.when(z < zs - 1)
    def _():
        right_copy(z, 0).start()

    @pl.when(z > 0)
    def _():
        left_copy(z, 0).start()

    k_copy(z, x).start()

    def pass_on(hop):
        @pl.when(z - hop >= 0)
        def _():
            right_copy(z - hop, hop - 1).wait_recv()

            @pl.when(z < zs - 1)
            def _():
                right_copy(z - hop, hop).start()

            x_copy(z - hop).start()
            k_copy(z - hop, x).start()

        @pl.when(z + hop < zs)
        def _():
            left_copy(z + hop, hop - 1).wait_recv()

            @pl.when(z > 0)
            def _():
                left_copy(z + hop, hop).start()

            x_copy(z + hop).start()
            k_copy(z + hop, x).start()

    def share(hop):
        def one(origin):
            x_copy(origin).wait_recv()
            k_copy(origin, 1 - x).start()

        if hop == 0:
            one(z)
            return

        @pl.when(z - hop >= 0)
        def _():
            one(z - hop)

        @pl.when(z + hop < zs)
        def _():
            one(z + hop)

    near = z < zs // 2
    groups = zs * 2 // clips_step
    rows = 2 * frames * HALF
    tile = col_tile(3 * width)
    tiles = 3 * width // tile
    parts = mod_ref.shape[0] // rows
    span_qkv = clips_step * group * qkv_rows
    span_out = clips_step * group * out_rows

    def take(origin):
        for x_of in range(2):
            k_copy(origin, x_of).wait_recv()

    def gather_group(index):
        for c in range(clips_step):
            clip_of = index * clips_step + c
            for g in range(group):
                slot = w_ref.at[clip_of // 2, clip_of % 2, g % 2]
                base = (g // 2) * shard_rows
                n = c * group + g
                stage_ref[n * qkv_rows : (n + 1) * qkv_rows, :] = slot[base : base + qkv_rows, :]
                stage_ref[span_qkv + n * out_rows : span_qkv + (n + 1) * out_rows, :] = slot[
                    base + qkv_rows : base + qkv_rows + out_rows, :
                ]
        wqkv_ref[pl.ds(pl.multiple_of(index * span_qkv, 16), span_qkv), :] = stage_ref[0:span_qkv, :]
        wout_ref[pl.ds(pl.multiple_of(index * span_out, 16), span_out), :] = stage_ref[
            span_qkv : span_qkv + span_out, :
        ]

    def columns(count_from, count_to):
        def one(step, carry):
            place = step // parts
            place = jnp.where(near, place, tiles - 1 - place)
            m = pl.multiple_of(lax.rem(step, parts) * rows, 16)
            n = pl.multiple_of(place * tile, 128)
            got = lax.dot_general(
                mod_ref[pl.ds(m, rows), :], wqkv_ref[pl.ds(n, tile), :], NT,
                preferred_element_type=jnp.float32,
            )
            qkv_ref[pl.ds(m, rows), pl.ds(n, tile)] = got.astype(jnp.bfloat16)
            return carry

        lax.fori_loop(count_from * parts, count_to * parts, one, 0)

    def advance(first, last, tile_from, tile_to):
        for ordinal in range(first, last):
            take(jnp.where(near, ordinal, zs - 1 - ordinal))
        begin, end = first * groups // zs, last * groups // zs

        def one(step, carry):
            gather_group(jnp.where(near, step, groups - 1 - step))
            return carry

        lax.fori_loop(begin, end, one, 0)
        columns(tile_from, tile_to)

    def modulate_all():
        own_x.wait()
        for step in range(1, group):
            in_copy(step).wait_recv()

        def first(step, carry):
            modulate_step(step, x_ref, table_ref, mod_ref)
            return carry

        lax.fori_loop(0, frames // 2 * blocks, first, 0)

    def ready(ordinals):
        return min(ordinals * groups // zs * span_qkv // tile, tiles)

    for hop in range(1, zs):
        pass_on(hop)
        share(hop - 1)
        if hop == zs // 2:
            modulate_all()
            advance(0, 1, 0, ready(1))
        if hop > zs // 2:
            advance(hop - zs // 2, hop - zs // 2 + 1, ready(hop - zs // 2), ready(hop - zs // 2 + 1))
    share(zs - 1)
    left = zs // 2
    for ordinal in range(left, zs):
        advance(ordinal, ordinal + 1, ready(ordinal), ready(ordinal + 1))

    def back_copy(step, block):
        to = mate(step)
        src = done_ref.at[pl.ds(to * own, own), pl.ds(pl.multiple_of(block * PAIR, PAIR), PAIR)]
        dst = out_ref.at[:, pl.ds(pl.multiple_of(grp * tokens + block * PAIR, PAIR), PAIR)]
        return remote(src, dst, back_send.at[step, block], back_recv.at[step, block], (clip, to))

    def back_own(block):
        src = done_ref.at[pl.ds(grp * own, own), pl.ds(pl.multiple_of(block * PAIR, PAIR), PAIR)]
        dst = out_ref.at[:, pl.ds(pl.multiple_of(grp * tokens + block * PAIR, PAIR), PAIR)]
        return pltpu.make_async_copy(src, dst, back_local.at[block])

    def third(block, carry):
        finish_block(block, x_ref, table_ref, length, qkv_ref, bias_ref, mixed_ref, proj_ref, wout_ref, done_ref)
        for step in range(1, group):
            back_copy(step, block).start()
        back_own(block).start()
        return carry

    lax.fori_loop(0, blocks, third, 0)

    for step in range(1, ys):
        y_copy(step).wait_send()
    for step in range(1, group):
        in_copy(step).wait_send()
    for hop in range(zs - 1):

        @pl.when((z - hop >= 0) & (z < zs - 1))
        def _():
            right_copy(z - hop, hop).wait_send()

        @pl.when((z + hop < zs) & (z > 0))
        def _():
            left_copy(z + hop, hop).wait_send()

    def sent(origin, carry):
        x_copy(origin).wait_send()
        for x_of in range(2):
            k_copy(origin, x_of).wait_send()
        return carry

    lax.fori_loop(0, zs, sent, 0)

    def returned(block, carry):
        for step in range(1, group):
            back_copy(step, block).wait_send()
            back_copy(step, block).wait_recv()
        back_own(block).wait()
        return carry

    lax.fori_loop(0, blocks, returned, 0)


def on_device(hidden, modulation, clip_frames, qkv_weight, out_weight):
    clips, group = lax.axis_size("clip"), lax.axis_size("grp")
    zs, ys = clips // 2, group // 2
    _, own, all_tokens, width = hidden.shape
    frames, tokens = own * group, all_tokens // group
    qkv_rows, out_rows = qkv_weight.shape[1], out_weight.shape[1]
    shard_rows = ceil16(qkv_rows + out_rows)
    clips_step = 1
    while clips_step * group * qkv_rows % 16 or clips_step * group * out_rows % 16:
        clips_step *= 2
    spare = jnp.zeros((shard_rows - qkv_rows - out_rows, width), jnp.bfloat16)
    shard = jnp.concatenate([qkv_weight.T, out_weight.T, spare], axis=0)
    rows = frames * HALF
    blocks = tokens // PAIR
    vmem = pl.BlockSpec(memory_space=pltpu.VMEM)
    hbm = pl.BlockSpec(memory_space=pl.ANY)
    dma = pltpu.SemaphoreType.DMA
    bf16 = jnp.bfloat16
    sizes = (zs, ys, group, shard_rows, qkv_rows, out_rows, clips_step)
    out = pl.pallas_call(
        functools.partial(kernel, sizes),
        out_shape=jax.ShapeDtypeStruct((own, all_tokens, width), bf16),
        in_specs=[pl.BlockSpec(memory_space=pltpu.SMEM), hbm, vmem, hbm],
        out_specs=hbm,
        scratch_shapes=[
            pltpu.VMEM((frames, tokens, width), bf16),
            pltpu.VMEM((zs, 2, 2, ys * shard_rows, width), bf16),
            pltpu.VMEM((clips_step * group * (qkv_rows + out_rows), width), bf16),
            pltpu.VMEM((3 * width, width), bf16),
            pltpu.VMEM((width, width), bf16),
            pltpu.VMEM((frames * tokens, width), bf16),
            pltpu.VMEM((frames * tokens, 3 * width), bf16),
            pltpu.VMEM((rows, rows), jnp.float32),
            pltpu.VMEM((2 * rows, width), bf16),
            pltpu.VMEM((2 * rows, width), jnp.float32),
            pltpu.VMEM((frames, tokens, width), bf16),
            dma((2,)), dma((ys,)), dma((ys,)),
            dma((zs,)), dma((zs,)), dma((zs,)), dma((zs,)),
            dma((zs,)), dma((zs,)), dma((2, zs)), dma((2, zs)),
            dma((group,)), dma((group,)), dma((group, blocks)), dma((group, blocks)), dma((blocks,)),
        ],
        compiler_params=pltpu.CompilerParams(
            collective_id=0, has_side_effects=True, vmem_limit_bytes=58 * 1024 * 1024
        ),
    )(clip_frames, hidden[0], modulation[0], shard)
    return out[None]


def solution(mesh):
    placed = (
        P("clip", "grp", None, None),
        P("clip", None, None),
        P("clip"),
        P(None, ("clip", "grp")),
        P(None, ("clip", "grp")),
    )
    return jax.shard_map(
        on_device,
        mesh=mesh,
        in_specs=placed,
        out_specs=P("clip", "grp", None, None),
        check_vma=False,
    )
```

```python
import functools

import jax
import jax.numpy as jnp
from jax import lax
from jax.experimental import pallas as pl
from jax.experimental.pallas import tpu as pltpu
from jax.sharding import PartitionSpec as P

HEADS = 16
HALF = 8
PAIR = 16
LOG2E = 1.4426950408889634
NT = (((1,), (1,)), ((), ()))


def col_tile(cols):
    return 384 if cols % 384 == 0 else 128


def make_bias(bias_ref, length):
    keys = bias_ref.shape[1]
    row = lax.broadcasted_iota(jnp.int32, bias_ref.shape, 0)
    col = lax.broadcasted_iota(jnp.int32, bias_ref.shape, 1)
    same = (row % HALF) == (col % HALF)
    live = (col // HALF) < length
    bias_ref[...] = jnp.where(same & live, 0.0, -1e30).astype(jnp.float32)


def modulate_step(step, x_ref, table_ref, mod_ref):
    frames, tokens, width = x_ref.shape
    pairs = frames // 2
    block = step // pairs
    pair = step % pairs
    x = x_ref[pl.ds(2 * pair, 2), pl.ds(PAIR * block, PAIR), :].astype(jnp.float32)
    mean = jnp.sum(x, axis=-1, keepdims=True) * (1.0 / width)
    centred = x - mean
    var = jnp.sum(centred * centred, axis=-1, keepdims=True) * (1.0 / width)
    normed = centred * lax.rsqrt(var + 1e-06)
    y = normed * (1.0 + table_ref[1:2, :])[None] + table_ref[0:1, :][None]
    for half in range(2):
        part = y[:, half * HALF : (half + 1) * HALF, :].reshape(2 * HALF, width)
        start = pl.multiple_of((2 * block + half) * frames * HALF + pair * 2 * HALF, 16)
        mod_ref[pl.ds(start, 2 * HALF), :] = part.astype(jnp.bfloat16)


def qkv_step(step, mod_ref, wqkv_ref, qkv_ref, rows, first=0):
    count = mod_ref.shape[0] // rows
    tile = col_tile(wqkv_ref.shape[0])
    n = pl.multiple_of((first + step // count) * tile, 128)
    m = pl.multiple_of((step % count) * rows, 16)
    got = lax.dot_general(
        mod_ref[pl.ds(m, rows), :], wqkv_ref[pl.ds(n, tile), :], NT,
        preferred_element_type=jnp.float32,
    )
    qkv_ref[pl.ds(m, rows), pl.ds(n, tile)] = got.astype(jnp.bfloat16)


def attend(start, rows, width, qkv_ref, bias_ref, mixed_ref, mixed_start):
    head = width // HEADS
    scale = head**-0.5 * LOG2E
    tiles = [None] * (width // 128)
    ones = jnp.ones((rows, 128), jnp.bfloat16)
    for h in range(HEADS):
        low, high = h * head, (h + 1) * head
        w0 = low // 128 * 128
        w1 = (high + 127) // 128 * 128
        lane = lax.broadcasted_iota(jnp.int32, (1, w1 - w0), 1) + w0
        inside = (lane >= low) & (lane < high)
        q = qkv_ref[pl.ds(start, rows), w0:w1]
        k = qkv_ref[pl.ds(start, rows), width + w0 : width + w1]
        v = qkv_ref[pl.ds(start, rows), 2 * width + w0 : 2 * width + w1]
        q = q * jnp.where(inside, 1.0, 0.0).astype(jnp.bfloat16)
        s = lax.dot_general(q, k, NT, preferred_element_type=jnp.float32)
        s = s * scale + bias_ref[...]
        p = jnp.exp2(s - jnp.max(s, axis=-1, keepdims=True))
        p = p.astype(jnp.bfloat16)
        total = jnp.dot(p, ones, preferred_element_type=jnp.float32)
        share = 1.0 / total
        o = jnp.dot(p, v, preferred_element_type=jnp.float32)
        for t in range(w0 // 128, w1 // 128):
            part = o[:, t * 128 - w0 : t * 128 - w0 + 128] * share
            where = inside[:, t * 128 - w0 : t * 128 - w0 + 128]
            tiles[t] = part if tiles[t] is None else jnp.where(where, part, tiles[t])
            if high >= (t + 1) * 128:
                mixed_ref[pl.ds(mixed_start, rows), t * 128 : (t + 1) * 128] = tiles[t].astype(
                    jnp.bfloat16
                )


def finish_block(block, x_ref, table_ref, length, qkv_ref, bias_ref, mixed_ref, proj_ref, wout_ref, out_ref):
    frames, tokens, width = x_ref.shape
    rows = frames * HALF

    def half_step(half, carry):
        start = pl.multiple_of((2 * block + half) * rows, 16)
        attend(start, rows, width, qkv_ref, bias_ref, mixed_ref, pl.multiple_of(half * rows, 16))
        return carry

    lax.fori_loop(0, 2, half_step, 0)
    tile = col_tile(width)
    def project(n, carry):
        at = pl.multiple_of(n * tile, 128)
        proj_ref[:, pl.ds(at, tile)] = lax.dot_general(
            mixed_ref[...], wout_ref[pl.ds(at, tile), :], NT, preferred_element_type=jnp.float32
        )
        return carry

    lax.fori_loop(0, width // tile, project, 0)
    gate = table_ref[2:3, :]

    def close(f, carry):
        at = pl.multiple_of(f * HALF, HALF)
        top = proj_ref[pl.ds(at, HALF), :]
        low = proj_ref[pl.ds(pl.multiple_of(rows + at, HALF), HALF), :]
        got = jnp.concatenate([top, low], axis=0)
        live = jnp.where(f < length, 1.0, 0.0).astype(jnp.float32)
        x = x_ref[f, pl.ds(pl.multiple_of(PAIR * block, PAIR), PAIR), :].astype(jnp.float32)
        out_ref[f, pl.ds(pl.multiple_of(PAIR * block, PAIR), PAIR), :] = (
            x + gate * got * live
        ).astype(jnp.bfloat16)
        return carry

    lax.fori_loop(0, frames, close, 0)


def ceil16(n):
    return (n + 15) // 16 * 16


def kernel(
    sizes, len_ref, hid_ref, table_ref, own_qkv_ref, own_out_ref, out_ref,
    x_ref, w_ref, stage_ref, wqkv_ref, wout_ref, mod_ref, qkv_ref, bias_ref, mixed_ref, proj_ref, done_ref,
    local_sem, y_send, y_recv, right_send, right_recv, left_send, left_recv, x_send, x_recv, k_send, k_recv,
    in_send, in_recv, back_send, back_recv, back_local,
):
    zs, ys, group, shard_rows, qkv_rows, out_rows, clips_step = sizes
    own, all_tokens, width = hid_ref.shape
    frames, tokens, _ = x_ref.shape
    blocks = tokens // PAIR
    clip, grp = lax.axis_index("clip"), lax.axis_index("grp")
    z, x = clip // 2, clip % 2
    y, k = grp // 2, grp % 2
    mesh_ids = pl.DeviceIdType.MESH
    length = len_ref[0]

    def mate(step):
        return lax.rem(grp + step, group)

    def at(z_to, x_to):
        return (z_to * 2 + x_to, grp)

    barrier = pltpu.get_barrier_semaphore()
    for step in range(1, group):
        pl.semaphore_signal(barrier, inc=1, device_id=(clip, mate(step)), device_id_type=mesh_ids)
    pl.semaphore_signal(barrier, inc=1, device_id=at(z, 1 - x), device_id_type=mesh_ids)

    @pl.when(z > 0)
    def _():
        pl.semaphore_signal(barrier, inc=1, device_id=at(z - 1, x), device_id_type=mesh_ids)

    @pl.when(z < zs - 1)
    def _():
        pl.semaphore_signal(barrier, inc=1, device_id=at(z + 1, x), device_id_type=mesh_ids)

    stage_ref[0:qkv_rows, :] = own_qkv_ref[...]
    stage_ref[qkv_rows : qkv_rows + out_rows, :] = own_out_ref[...]
    w_ref[z, x, k, pl.ds(pl.multiple_of(y * shard_rows, 16), shard_rows), :] = stage_ref[0:shard_rows, :]
    own_x = pltpu.make_async_copy(
        hid_ref.at[:, pl.ds(pl.multiple_of(grp * tokens, PAIR), tokens)],
        x_ref.at[pl.ds(grp * own, own)], local_sem.at[0],
    )
    own_x.start()
    ends = jnp.where(z > 0, 1, 0) + jnp.where(z < zs - 1, 1, 0)
    pl.semaphore_wait(barrier, group + ends)

    def remote(src, dst, send, recv, to):
        return pltpu.make_async_remote_copy(
            src_ref=src, dst_ref=dst, send_sem=send, recv_sem=recv, device_id=to, device_id_type=mesh_ids
        )

    def slot_of(origin, x_of, dy):
        rows = pl.multiple_of(lax.rem(y + dy, ys) * shard_rows, 16)
        return w_ref.at[origin, x_of, k, pl.ds(rows, shard_rows)]

    def y_copy(step):
        to = (clip, lax.rem(y + step, ys) * 2 + k)
        slot = slot_of(z, x, 0)
        return remote(slot, slot, y_send.at[step], y_recv.at[step], to)

    def in_copy(step):
        to = mate(step)
        src = hid_ref.at[:, pl.ds(pl.multiple_of(to * tokens, PAIR), tokens)]
        return remote(src, x_ref.at[pl.ds(grp * own, own)], in_send.at[step], in_recv.at[step], (clip, to))

    def right_copy(origin, hop, dy):
        slot = slot_of(origin, x, dy)
        return remote(slot, slot, right_send.at[hop, dy], right_recv.at[hop, dy], at(z + 1, x))

    def left_copy(origin, hop, dy):
        slot = slot_of(origin, x, dy)
        return remote(slot, slot, left_send.at[hop, dy], left_recv.at[hop, dy], at(z - 1, x))

    def x_copy(origin, dy):
        slot = slot_of(origin, x, dy)
        return remote(slot, slot, x_send.at[origin, dy], x_recv.at[origin, dy], at(z, 1 - x))

    def k_copy(origin, x_of, dy):
        slot = slot_of(origin, x_of, dy)
        to = (clip, y * 2 + 1 - k)
        return remote(slot, slot, k_send.at[x_of, origin, dy], k_recv.at[x_of, origin, dy], to)

    def begin(dy):
        x_copy(z, dy).start()

        @pl.when(z < zs - 1)
        def _():
            right_copy(z, 0, dy).start()

        @pl.when(z > 0)
        def _():
            left_copy(z, 0, dy).start()

        k_copy(z, x, dy).start()

    for step in range(1, ys):
        y_copy(step).start()
    begin(0)
    make_bias(bias_ref, length)
    for step in range(1, ys):
        y_copy(step).wait_recv()
        begin(ys - step)
    for step in range(1, group):
        in_copy(step).start()

    def pass_on(hop):
        for dy in range(ys):

            @pl.when(z - hop >= 0)
            def _():
                right_copy(z - hop, hop - 1, dy).wait_recv()
                x_copy(z - hop, dy).start()

                @pl.when(z < zs - 1)
                def _():
                    right_copy(z - hop, hop, dy).start()

                k_copy(z - hop, x, dy).start()

            @pl.when(z + hop < zs)
            def _():
                left_copy(z + hop, hop - 1, dy).wait_recv()
                x_copy(z + hop, dy).start()

                @pl.when(z > 0)
                def _():
                    left_copy(z + hop, hop, dy).start()

                k_copy(z + hop, x, dy).start()

    def share(hop):
        for dy in range(ys):

            def one(origin):
                x_copy(origin, dy).wait_recv()
                k_copy(origin, 1 - x, dy).start()

            if hop == 0:
                one(z)
                continue

            @pl.when(z - hop >= 0)
            def _():
                one(z - hop)

            @pl.when(z + hop < zs)
            def _():
                one(z + hop)

    near = z < zs // 2
    groups = zs * 2 // clips_step
    rows = 2 * frames * HALF
    tile = col_tile(3 * width)
    tiles = 3 * width // tile
    parts = mod_ref.shape[0] // rows
    span_qkv = clips_step * group * qkv_rows
    span_out = clips_step * group * out_rows

    def take(origin):
        for x_of in range(2):
            for dy in range(ys):
                k_copy(origin, x_of, dy).wait_recv()

    def gather_group(index):
        for c in range(clips_step):
            clip_of = index * clips_step + c
            for g in range(group):
                slot = w_ref.at[clip_of // 2, clip_of % 2, g % 2]
                base = (g // 2) * shard_rows
                n = c * group + g
                stage_ref[n * qkv_rows : (n + 1) * qkv_rows, :] = slot[base : base + qkv_rows, :]
                stage_ref[span_qkv + n * out_rows : span_qkv + (n + 1) * out_rows, :] = slot[
                    base + qkv_rows : base + qkv_rows + out_rows, :
                ]
        wqkv_ref[pl.ds(pl.multiple_of(index * span_qkv, 16), span_qkv), :] = stage_ref[0:span_qkv, :]
        wout_ref[pl.ds(pl.multiple_of(index * span_out, 16), span_out), :] = stage_ref[
            span_qkv : span_qkv + span_out, :
        ]

    def columns(count_from, count_to):
        def one(step, carry):
            place = step // parts
            place = jnp.where(near, place, tiles - 1 - place)
            m = pl.multiple_of(lax.rem(step, parts) * rows, 16)
            n = pl.multiple_of(place * tile, 128)
            got = lax.dot_general(
                mod_ref[pl.ds(m, rows), :], wqkv_ref[pl.ds(n, tile), :], NT,
                preferred_element_type=jnp.float32,
            )
            qkv_ref[pl.ds(m, rows), pl.ds(n, tile)] = got.astype(jnp.bfloat16)
            return carry

        lax.fori_loop(count_from * parts, count_to * parts, one, 0)

    def advance(first, last, tile_from, tile_to):
        for ordinal in range(first, last):
            take(jnp.where(near, ordinal, zs - 1 - ordinal))
        begin, end = first * groups // zs, last * groups // zs

        def one(step, carry):
            gather_group(jnp.where(near, step, groups - 1 - step))
            return carry

        lax.fori_loop(begin, end, one, 0)
        columns(tile_from, tile_to)

    def modulate_all():
        own_x.wait()
        for step in range(1, group):
            in_copy(step).wait_recv()

        def first(step, carry):
            modulate_step(step, x_ref, table_ref, mod_ref)
            return carry

        lax.fori_loop(0, frames // 2 * blocks, first, 0)

    def ready(ordinals):
        return min(ordinals * groups // zs * span_qkv // tile, tiles)

    for hop in range(1, zs):
        pass_on(hop)
        share(hop - 1)
    modulate_all()
    for ordinal in range(zs):
        if ordinal == zs - 1:
            share(zs - 1)
        advance(ordinal, ordinal + 1, ready(ordinal), ready(ordinal + 1))

    def back_copy(step, block):
        to = mate(step)
        src = done_ref.at[pl.ds(to * own, own), pl.ds(pl.multiple_of(block * PAIR, PAIR), PAIR)]
        dst = out_ref.at[:, pl.ds(pl.multiple_of(grp * tokens + block * PAIR, PAIR), PAIR)]
        return remote(src, dst, back_send.at[step, block], back_recv.at[step, block], (clip, to))

    def back_own(block):
        src = done_ref.at[pl.ds(grp * own, own), pl.ds(pl.multiple_of(block * PAIR, PAIR), PAIR)]
        dst = out_ref.at[:, pl.ds(pl.multiple_of(grp * tokens + block * PAIR, PAIR), PAIR)]
        return pltpu.make_async_copy(src, dst, back_local.at[block])

    def third(block, carry):
        finish_block(block, x_ref, table_ref, length, qkv_ref, bias_ref, mixed_ref, proj_ref, wout_ref, done_ref)
        for step in range(1, group):
            back_copy(step, block).start()
        back_own(block).start()
        return carry

    lax.fori_loop(0, blocks, third, 0)

    for step in range(1, ys):
        y_copy(step).wait_send()
    for step in range(1, group):
        in_copy(step).wait_send()
    for hop in range(zs - 1):

        @pl.when((z - hop >= 0) & (z < zs - 1))
        def _():
            for dy in range(ys):
                right_copy(z - hop, hop, dy).wait_send()

        @pl.when((z + hop < zs) & (z > 0))
        def _():
            for dy in range(ys):
                left_copy(z + hop, hop, dy).wait_send()

    def sent(origin, carry):
        for dy in range(ys):
            x_copy(origin, dy).wait_send()
            for x_of in range(2):
                k_copy(origin, x_of, dy).wait_send()
        return carry

    lax.fori_loop(0, zs, sent, 0)

    def returned(block, carry):
        for step in range(1, group):
            back_copy(step, block).wait_send()
            back_copy(step, block).wait_recv()
        back_own(block).wait()
        return carry

    lax.fori_loop(0, blocks, returned, 0)


def on_device(hidden, modulation, clip_frames, qkv_weight, out_weight):
    clips, group = lax.axis_size("clip"), lax.axis_size("grp")
    zs, ys = clips // 2, group // 2
    _, own, all_tokens, width = hidden.shape
    frames, tokens = own * group, all_tokens // group
    qkv_rows, out_rows = qkv_weight.shape[1], out_weight.shape[1]
    shard_rows = ceil16(qkv_rows + out_rows)
    clips_step = 1
    while clips_step * group * qkv_rows % 16 or clips_step * group * out_rows % 16:
        clips_step *= 2
    rows = frames * HALF
    blocks = tokens // PAIR
    vmem = pl.BlockSpec(memory_space=pltpu.VMEM)
    hbm = pl.BlockSpec(memory_space=pl.ANY)
    dma = pltpu.SemaphoreType.DMA
    bf16 = jnp.bfloat16
    sizes = (zs, ys, group, shard_rows, qkv_rows, out_rows, clips_step)
    out = pl.pallas_call(
        functools.partial(kernel, sizes),
        out_shape=jax.ShapeDtypeStruct((own, all_tokens, width), bf16),
        in_specs=[pl.BlockSpec(memory_space=pltpu.SMEM), hbm, vmem, vmem, vmem],
        out_specs=hbm,
        scratch_shapes=[
            pltpu.VMEM((frames, tokens, width), bf16),
            pltpu.VMEM((zs, 2, 2, ys * shard_rows, width), bf16),
            pltpu.VMEM((clips_step * group * (qkv_rows + out_rows), width), bf16),
            pltpu.VMEM((3 * width, width), bf16),
            pltpu.VMEM((width, width), bf16),
            pltpu.VMEM((frames * tokens, width), bf16),
            pltpu.VMEM((frames * tokens, 3 * width), bf16),
            pltpu.VMEM((rows, rows), jnp.float32),
            pltpu.VMEM((2 * rows, width), bf16),
            pltpu.VMEM((2 * rows, width), jnp.float32),
            pltpu.VMEM((frames, tokens, width), bf16),
            dma((1,)), dma((ys,)), dma((ys,)),
            dma((zs, ys)), dma((zs, ys)), dma((zs, ys)), dma((zs, ys)),
            dma((zs, ys)), dma((zs, ys)), dma((2, zs, ys)), dma((2, zs, ys)),
            dma((group,)), dma((group,)), dma((group, blocks)), dma((group, blocks)), dma((blocks,)),
        ],
        compiler_params=pltpu.CompilerParams(
            collective_id=0, has_side_effects=True, vmem_limit_bytes=58 * 1024 * 1024
        ),
    )(clip_frames, hidden[0], modulation[0], qkv_weight.T, out_weight.T)
    return out[None]


def solution(mesh):
    placed = (
        P("clip", "grp", None, None),
        P("clip", None, None),
        P("clip"),
        P(None, ("clip", "grp")),
        P(None, ("clip", "grp")),
    )
    return jax.shard_map(
        on_device,
        mesh=mesh,
        in_specs=placed,
        out_specs=P("clip", "grp", None, None),
        check_vma=False,
    )
```
